32 devices in a mesh: groups: 2 (over y), expert: 8 (over z, core), dp: 2 (over x).
Axes of the slice: x: 2, y: 2, z: 4, core: 2. Of those that a mesh axis runs over, the one named last changes fastest.
Arguments:
- tokens: bfloat16 [4096, 2048], P(('groups', 'expert', 'dp')), parts along dimension 0, may hold values from -6 to 6
- expert_ids: int32 [4096, 8], P(('groups', 'expert', 'dp')), parts along dimension 0, may hold values from 0 to 15, all different within a row; in each aligned block of 128 rows (0 to 127, 128 to 255, ...) at most 72 rows name the same one
- gate_weights: bfloat16 [4096, 8], P(('groups', 'expert', 'dp')), parts along dimension 0, may hold values from 0.049804688 to 0.5
- cotangent: bfloat16 [4096, 2048], P(('groups', 'expert', 'dp')), parts along dimension 0, may hold values from -0.796875 to 0.796875
- gate_matrix: bfloat16 [16, 2048, 384], P('expert', 'dp'), may hold values from -0.125 to 0.125
- up_weight: bfloat16 [16, 2048, 384], P('expert', 'dp'), may hold values from -0.125 to 0.125
- down_weight: bfloat16 [16, 384, 2048], P('expert', None, 'dp'), may hold values from -0.3125 to 0.3125
Outputs:
- grad_tokens: bfloat16 [4096, 2048], P(('groups', 'expert', 'dp')), parts along dimension 0
- grad_gates: bfloat16 [4096, 8], P(('groups', 'expert', 'dp')), parts along dimension 0
- grad_gate_matrix: bfloat16 [32, 2048, 384], P(('groups', 'expert'), 'dp'), parts along dimension 0
- grad_up: bfloat16 [32, 2048, 384], P(('groups', 'expert'), 'dp'), parts along dimension 0
- grad_down: bfloat16 [32, 384, 2048], P(('groups', 'expert'), None, 'dp'), parts along dimension 0
The draws below stay inside these ranges and needn't reach their ends.
There are 2 independent parts, one for each index of `groups`. The reference program is written for one: setup_inputs(seed, part) draws one part's arguments, and reference() takes and returns one part's arrays. A program takes and returns all parts, laid end to end along the dimension named above; an argument that names none is the same for every part. Nothing has to cross between parts.
Inputs may be any that keep to these rules, and one draw needn't show every extreme that they name: `expert_ids`: each row names 8 different experts; among the 128 tokens of one device no expert is named more than 72 times, and in every draw some expert is named exactly 72 times by the tokens of some device.
All inputs are finite; a program needn't handle non-finite values.
Results may differ from the reference program's by a relative error of at most 0.008.
Values may be sent and summed in bfloat16 or wider, within the bound.
A program may use at most 128 MiB of HBM per device.

```python
import math
import jax
import jax.numpy as jnp
import numpy as np
from jax import lax

D = 2048
FF = 384
TOP = 8
TOK_DEV = 128
EXPERTS = 16
CAP = 72
TOKENS = 2048
N_EXPERT = 8
N_DP = 2


def block_scale(key, shape, cuts, least, largest):
    gain, own = 1.0, jax.random.fold_in(key, 6)
    for dim, blocks in cuts:
        draws = jnp.exp(jax.random.uniform(jax.random.fold_in(own, dim), (blocks,), jnp.float32, least / len(cuts), largest / len(cuts)))
        gain = gain * jnp.repeat(draws, shape[dim] // blocks).reshape([-1 if axis == dim else 1 for axis in range(len(shape))])
    return gain


def deal_out(stream_key, own, number, rows, number_of, top, bound, lean):
    ranking = jax.random.permutation(stream_key, number_of)
    crowded, common = portions_of(number_of, rows * top, bound, lean, True), portions_of(number_of, rows * top, bound, lean, False)
    places = jnp.arange(number_of)

    def named(lengths, turn):
        used = int((lengths > 0).sum())
        fixed = max(1, used // 4)
        moved = fixed + (places - fixed + turn * (used - fixed)) % max(1, number_of - fixed)
        return jnp.zeros((number_of,), jnp.int32).at[ranking[jnp.where(places < fixed, places, moved)]].set(jnp.asarray(lengths, jnp.int32))

    lengths = jnp.where(number % 4 == 0, named(crowded, number // 4), named(common, number - number // 4 - 1))
    mixed = jax.random.permutation(jax.random.fold_in(own, 3), number_of)
    donor, taker = mixed[0:number_of // 2 * 2:2], mixed[1:number_of // 2 * 2:2]
    slack = jnp.minimum(lengths[donor] - 1, bound - lengths[taker]) // 2
    slack = jnp.where((donor == ranking[0]) | (taker == ranking[0]) | (lengths[taker] == 0), 0, jnp.maximum(slack, 0))
    moved = jax.random.randint(jax.random.fold_in(own, 4), (number_of // 2,), 0, 1 << 20) % (slack + 1)
    lengths = lengths.at[donor].add(-moved).at[taker].add(moved)
    labels = jnp.searchsorted(jnp.cumsum(lengths), jnp.arange(rows * top), side="right").astype(jnp.int32)
    table = labels.reshape(top, rows).T
    table = table[jax.random.permutation(jax.random.fold_in(own, 1), rows)]
    turn = jax.random.randint(jax.random.fold_in(own, 2), (rows, 1), 0, top)
    return jnp.take_along_axis(table, (jnp.arange(top)[None, :] + turn) % top, axis=1)


def portions_of(number_of, total, most, lean, full):
    weights = [(1 << 20) // math.isqrt(standing ** lean) + 1 for standing in range(1, number_of + 1)]
    largest = most if full else min(most, max(-(-total // number_of), total * weights[0] // sum(weights)))
    least = 1 if total - largest >= number_of - 1 else 0
    given, surplus = [largest] + [least] * (number_of - 1), total - largest - least * (number_of - 1)
    while surplus > 0:
        free = [i for i in range(1, number_of) if given[i] < largest] or [i for i in range(1, number_of) if given[i] < most]
        mass, left = sum([weights[i] for i in free]), surplus
        for i in free:
            extra = min(most - given[i], max(1, left * weights[i] // mass), surplus)
            given[i] = given[i] + extra
            surplus = surplus - extra
    return np.array(given)


def scatter_about(key, dims, deviation, limit, split=(), held_as=jnp.bfloat16):
    array = jax.random.normal(key, dims, jnp.float32) * deviation
    if len(split) > 0:
        array = block_scale(key, dims, split, -0.22, 0.18) * array
    return jnp.clip(array, min=-limit, max=limit).astype(held_as)


def setup_inputs(seed: int = 0, part: int = 0) -> dict:
    streams_of = jax.random.split(jax.random.key(seed), 8)
    part_splits = jax.random.split(jax.random.fold_in(streams_of[7], part), 8)
    tokens = scatter_about(part_splits[0], (TOKENS, D), 1.0, 6.0, ((0, 16),))
    expert_ids_keys = jax.random.split(jax.random.fold_in(part_splits[1], 1), TOKENS // TOK_DEV)
    expert_ids_turns = jax.random.permutation(jax.random.fold_in(part_splits[1], 3), TOKENS // TOK_DEV)
    expert_ids = jax.vmap(lambda own, number: deal_out(jax.random.fold_in(part_splits[1], 2), own, number, TOK_DEV, EXPERTS, TOP, CAP, 2))(expert_ids_keys, expert_ids_turns).reshape((TOKENS, TOP))
    gate_weights = jnp.clip(jnp.exp(math.log(0.5) - 2.306499 * jax.random.uniform(part_splits[2], (TOKENS, TOP), jnp.float32) ** block_scale(part_splits[2], (TOKENS, TOP), ((0, 16),), -0.2, 0.2)), 0.049804688, 0.5).astype(jnp.bfloat16)
    cotangent = scatter_about(part_splits[3], (TOKENS, D), 0.1, 0.796875, ((0, 16),))
    gate_matrix = scatter_about(streams_of[4], (EXPERTS, D, FF), D ** -0.5, 0.125, ((0, 8), (1, 2)))
    up_weight = scatter_about(streams_of[5], (EXPERTS, D, FF), D ** -0.5, 0.125, ((0, 8), (1, 2)))
    down_weight = scatter_about(streams_of[6], (EXPERTS, FF, D), FF ** -0.5, 0.3125, ((0, 8), (2, 2)))
    return {"tokens": tokens, "expert_ids": expert_ids, "gate_weights": gate_weights, "cotangent": cotangent, "gate_matrix": gate_matrix, "up_weight": up_weight, "down_weight": down_weight}


def grouped_sum(first_rows, second_rows):
    first = first_rows.reshape(N_EXPERT, N_DP, CAP, first_rows.shape[1]).astype(jnp.float32)
    second = second_rows.reshape(N_EXPERT, N_DP, CAP, second_rows.shape[1]).astype(jnp.float32)
    partial_sums = jnp.einsum("ejcd,ejcf->jdf", first, second, precision=lax.Precision.HIGHEST)
    partial_sums = lax.optimization_barrier(partial_sums.astype(jnp.bfloat16))
    return jnp.sum(partial_sums.astype(jnp.float32), axis=0).astype(jnp.bfloat16)


def reference(tokens, expert_ids, gate_weights, cotangent, gate_matrix, up_weight, down_weight):
    devices = N_EXPERT * N_DP
    pairs = TOK_DEV * TOP
    ids = expert_ids.reshape(devices, pairs)
    onehot = (ids[:, :, None] == jnp.arange(EXPERTS, dtype=jnp.int32)[None, None, :]).astype(jnp.int32)
    before = jnp.cumsum(onehot, axis=1) - onehot
    position = jnp.sum(before * onehot, axis=2).astype(jnp.int32)
    slot = (ids * CAP + position).astype(jnp.int32)
    global_pair = jnp.arange(devices * pairs, dtype=jnp.int32).reshape(devices, pairs)
    row_select = jnp.broadcast_to(jnp.arange(devices, dtype=jnp.int32)[:, None], (devices, pairs))
    owner = jnp.full((devices, EXPERTS * CAP), -1, jnp.int32).at[row_select, slot].set(global_pair)
    owner = owner.reshape(devices, EXPERTS, CAP).transpose(1, 0, 2).reshape(EXPERTS, devices * CAP)
    flat_gate = gate_weights.reshape(-1)

    def one_expert(carry, inputs):
        acc_rows, acc_gate = carry
        index, w_gate, w_up, w_down = inputs
        filled = index >= 0
        safe = jnp.maximum(index, 0)
        token_row = safe // TOP
        rows = jnp.where(filled[:, None], tokens[token_row], jnp.zeros((), tokens.dtype))
        grads = jnp.where(filled[:, None], cotangent[token_row], jnp.zeros((), cotangent.dtype))
        gate = jnp.where(filled, flat_gate[safe], jnp.zeros((), flat_gate.dtype)).astype(jnp.float32)[:, None]
        pre_gate = jnp.dot(rows, w_gate, preferred_element_type=jnp.float32)
        pre_up = jnp.dot(rows, w_up, preferred_element_type=jnp.float32)
        sig = jax.nn.sigmoid(pre_gate)
        active = pre_gate * sig
        hidden = lax.optimization_barrier((active * pre_up).astype(jnp.bfloat16))
        back = jnp.dot(grads, w_down.T, preferred_element_type=jnp.float32)
        gate_grad = jnp.sum(hidden.astype(jnp.float32) * back, axis=1).astype(jnp.bfloat16)
        d_hidden = gate * back
        d_gate = (d_hidden * pre_up * (sig * (1.0 + pre_gate * (1.0 - sig)))).astype(jnp.bfloat16)
        d_up = (d_hidden * active).astype(jnp.bfloat16)
        d_out = (gate * grads.astype(jnp.float32)).astype(jnp.bfloat16)
        both = jnp.dot(d_gate, w_gate.T, preferred_element_type=jnp.float32) + jnp.dot(d_up, w_up.T, preferred_element_type=jnp.float32)
        d_rows = lax.optimization_barrier(both.astype(jnp.bfloat16))
        grad_gate_e = grouped_sum(rows, d_gate)
        grad_up_e = grouped_sum(rows, d_up)
        grad_down_e = grouped_sum(hidden, d_out)
        target = jnp.where(filled, safe, devices * pairs).astype(jnp.int32)
        acc_rows = acc_rows.at[target // TOP].add(d_rows.astype(jnp.float32), mode="drop")
        acc_gate = acc_gate.at[target].set(gate_grad, mode="drop")
        return (acc_rows, acc_gate), (grad_gate_e, grad_up_e, grad_down_e)

    start = (jnp.zeros((TOKENS, D), jnp.float32), jnp.zeros((TOKENS * TOP,), jnp.bfloat16))
    (acc_rows, acc_gate), (grad_gate, grad_up, grad_down) = lax.scan(one_expert, start, (owner, gate_matrix, up_weight, down_weight))
    return acc_rows.astype(jnp.bfloat16), acc_gate.reshape(TOKENS, TOP), grad_gate, grad_up, grad_down
```

```python
import jax
import jax.numpy as jnp
from jax import lax
from jax.sharding import PartitionSpec as P

F32 = jnp.float32
BF16 = jnp.bfloat16


def mm(a, b, dims):
    return lax.dot_general(a, b, (dims, ((), ())), preferred_element_type=F32)


def dispatch_body(tokens, expert_ids, gate_weights, cotangent, gate_matrix, up_weight, down_weight):
    tok_dev, top = expert_ids.shape
    exp_dev = up_weight.shape[0]
    n_peers = lax.axis_size("expert")
    experts = exp_dev * n_peers
    cap = min(tok_dev, tok_dev * top * 9 // (8 * experts))
    width = tokens.shape[1]
    flat_ids = expert_ids.reshape(-1)
    pairs = flat_ids.shape[0]
    onehot = (flat_ids[:, None] == jnp.arange(experts, dtype=jnp.int32)[None, :]).astype(jnp.int32)
    before = jnp.cumsum(onehot, axis=0) - onehot
    position = jnp.sum(before * onehot, axis=1)
    slot = flat_ids * cap + position
    owner = (
        jnp.full((experts * cap,), -1, jnp.int32).at[slot].set(jnp.arange(pairs, dtype=jnp.int32))
    )
    filled = owner >= 0
    safe_pair = jnp.maximum(owner, 0)
    token_row = safe_pair // top
    send_rows = jnp.where(filled[:, None], tokens[token_row], jnp.zeros((), tokens.dtype)).reshape(
        n_peers, exp_dev * cap, width
    )
    send_gate = jnp.where(
        filled, gate_weights.reshape(-1)[safe_pair], jnp.zeros((), gate_weights.dtype)
    ).reshape(n_peers, exp_dev * cap)
    send_grad = jnp.where(
        filled[:, None], cotangent[token_row], jnp.zeros((), cotangent.dtype)
    ).reshape(n_peers, exp_dev * cap, width)
    recv_rows, recv_gate = (
        lax.all_to_all(send_rows, "expert", split_axis=0, concat_axis=0, tiled=True),
        lax.all_to_all(send_gate, "expert", split_axis=0, concat_axis=0, tiled=True),
    )
    full_gate, full_up, full_down = (
        lax.all_gather(gate_matrix, "dp", axis=1, tiled=True),
        lax.all_gather(up_weight, "dp", axis=1, tiled=True),
        lax.all_gather(down_weight, "dp", axis=2, tiled=True),
    )
    rows_four = recv_rows.reshape(n_peers, exp_dev, cap, width)
    pre_gate = jnp.einsum(
        "slcd,ldf->slcf", rows_four, full_gate, preferred_element_type=jnp.float32
    )
    pre_up = jnp.einsum("slcd,ldf->slcf", rows_four, full_up, preferred_element_type=jnp.float32)
    sig = jax.nn.sigmoid(pre_gate)
    active = pre_gate * sig
    hidden = (active * pre_up).astype(jnp.bfloat16)
    recv_grad = lax.all_to_all(send_grad, "expert", split_axis=0, concat_axis=0, tiled=True)
    grad_four = recv_grad.reshape(n_peers, exp_dev, cap, width)
    gate_three = recv_gate.reshape(n_peers, exp_dev, cap).astype(jnp.float32)[..., None]
    back = jnp.einsum("slcd,lfd->slcf", grad_four, full_down, preferred_element_type=jnp.float32)
    gate_grad = jnp.sum(hidden.astype(jnp.float32) * back, axis=3).astype(jnp.bfloat16)
    d_hidden = gate_three * back
    d_gate = (d_hidden * pre_up * (sig * (1.0 + pre_gate * (1.0 - sig)))).astype(jnp.bfloat16)
    d_up = (d_hidden * active).astype(jnp.bfloat16)
    d_out = (gate_three * grad_four.astype(jnp.float32)).astype(jnp.bfloat16)
    both = jnp.einsum("slcf,ldf->slcd", d_gate, full_gate, preferred_element_type=jnp.float32)
    both = both + jnp.einsum("slcf,ldf->slcd", d_up, full_up, preferred_element_type=jnp.float32)
    d_rows = both.astype(jnp.bfloat16)
    ret_rows, ret_gate = (
        lax.all_to_all(
            d_rows.reshape(n_peers, exp_dev * cap, width),
            "expert",
            split_axis=0,
            concat_axis=0,
            tiled=True,
        ),
        lax.all_to_all(
            gate_grad.reshape(n_peers, exp_dev * cap),
            "expert",
            split_axis=0,
            concat_axis=0,
            tiled=True,
        ),
    )
    gate_term = jnp.einsum("slcd,slcf->ldf", rows_four, d_gate, preferred_element_type=jnp.float32)
    up_term = jnp.einsum("slcd,slcf->ldf", rows_four, d_up, preferred_element_type=jnp.float32)
    down_term = jnp.einsum("slcf,slcd->lfd", hidden, d_out, preferred_element_type=jnp.float32)
    gate_sum, up_sum, down_sum = (
        lax.psum_scatter(
            gate_term.astype(jnp.bfloat16), "dp", scatter_dimension=1, tiled=True
        ).astype(jnp.float32),
        lax.psum_scatter(
            up_term.astype(jnp.bfloat16), "dp", scatter_dimension=1, tiled=True
        ).astype(jnp.float32),
        lax.psum_scatter(
            down_term.astype(jnp.bfloat16), "dp", scatter_dimension=2, tiled=True
        ).astype(jnp.float32),
    )
    per_pair = ret_rows.reshape(experts * cap, width)[slot]
    grad_tokens = jnp.sum(per_pair.reshape(tok_dev, top, width).astype(jnp.float32), axis=1).astype(
        jnp.bfloat16
    )
    grad_gates = ret_gate.reshape(-1)[slot].reshape(tok_dev, top)
    return (
        grad_tokens,
        grad_gates,
        gate_sum.astype(jnp.bfloat16),
        up_sum.astype(jnp.bfloat16),
        down_sum.astype(jnp.bfloat16),
    )


def dense_body(tokens, expert_ids, gate_weights, cotangent, gate_matrix, up_weight, down_weight):
    tok_dev, top = expert_ids.shape
    width = tokens.shape[1]
    exp_dev, _, ff = up_weight.shape
    n_peers = lax.axis_size("expert")
    experts = exp_dev * n_peers
    me = lax.axis_index("expert")
    rows = tok_dev * n_peers

    chosen = expert_ids[:, :, None] == jnp.arange(experts, dtype=jnp.int32)[None, None, :]
    dense = jnp.sum(jnp.where(chosen, gate_weights[:, :, None].astype(F32), 0.0), axis=1)
    dense = dense.astype(BF16)

    x = lax.all_gather(tokens, "expert", axis=0, tiled=True)
    full_gate = lax.all_gather(gate_matrix, "dp", axis=1, tiled=True)
    full_up = lax.all_gather(up_weight, "dp", axis=1, tiled=True)
    c = lax.all_gather(cotangent, "expert", axis=0, tiled=True)
    full_down = lax.all_gather(down_weight, "dp", axis=2, tiled=True)
    gates = lax.all_gather(dense, "expert", axis=0, tiled=True)
    mine = lax.dynamic_slice_in_dim(gates, me * exp_dev, exp_dev, axis=1).astype(F32)

    d_gates, d_ups, weighted, gate_grads = [], [], [], []
    for e in range(exp_dev):
        g = mine[:, e : e + 1]
        pre_gate = mm(x, full_gate[e], ((1,), (0,)))
        pre_up = mm(x, full_up[e], ((1,), (0,)))
        sig = jax.nn.sigmoid(pre_gate)
        active = pre_gate * sig
        hidden = (active * pre_up).astype(BF16).astype(F32)
        back = mm(c, full_down[e], ((1,), (1,)))
        gate_grads.append(jnp.sum(hidden * back, axis=1, keepdims=True))
        d_hidden = g * back
        d_gates.append((d_hidden * pre_up * (sig * (1.0 + pre_gate * (1.0 - sig)))).astype(BF16))
        d_ups.append((d_hidden * active).astype(BF16))
        weighted.append((g * hidden).astype(BF16))

    def scatter(term, dim):
        return lax.psum_scatter(term.astype(BF16), "dp", scatter_dimension=dim, tiled=True)

    gate_out = scatter(jnp.stack([mm(x, d, ((0,), (0,))) for d in d_gates]), 1)
    up_out = scatter(jnp.stack([mm(x, d, ((0,), (0,))) for d in d_ups]), 1)
    down_out = scatter(jnp.stack([mm(h, c, ((0,), (0,))) for h in weighted]), 2)

    both = sum(mm(d_gates[e], full_gate[e], ((1,), (1,))) for e in range(exp_dev))
    both = both + sum(mm(d_ups[e], full_up[e], ((1,), (1,))) for e in range(exp_dev))
    gg = jnp.concatenate(gate_grads, axis=1).astype(BF16)
    grad_tokens = lax.psum_scatter(both.astype(BF16), "expert", scatter_dimension=0, tiled=True)
    back_gate = lax.all_to_all(
        gg.reshape(n_peers, tok_dev, exp_dev), "expert", split_axis=0, concat_axis=0, tiled=True
    )
    back_gate = back_gate.transpose(1, 0, 2).reshape(tok_dev, experts)
    grad_gates = jnp.sum(
        jnp.where(chosen, back_gate[:, None, :].astype(F32), 0.0), axis=2
    ).astype(BF16)
    return grad_tokens, grad_gates, gate_out, up_out, down_out


def body(*args):
    tok_dev, top = args[1].shape
    experts = args[5].shape[0] * lax.axis_size("expert")
    cap = min(tok_dev, tok_dev * top * 9 // (8 * experts))
    dense = tok_dev <= 2 * cap
    return (dense_body if dense else dispatch_body)(*args)


def solution(mesh):
    placed = (
        P(("groups", "expert", "dp"), None),
        P(("groups", "expert", "dp"), None),
        P(("groups", "expert", "dp"), None),
        P(("groups", "expert", "dp"), None),
        P("expert", "dp", None),
        P("expert", "dp", None),
        P("expert", None, "dp"),
    )
    return jax.shard_map(
        body,
        mesh=mesh,
        in_specs=placed,
        out_specs=(
            P(("groups", "expert", "dp"), None),
            P(("groups", "expert", "dp"), None),
            P(("groups", "expert"), "dp", None),
            P(("groups", "expert"), "dp", None),
            P(("groups", "expert"), None, "dp"),
        ),
        check_vma=False,
    )
```

```python
import jax
import jax.numpy as jnp
from jax import lax
from jax.experimental import pallas as pl
from jax.experimental.pallas import tpu as pltpu
from jax.sharding import PartitionSpec as P

F32 = jnp.float32
BF16 = jnp.bfloat16


MESH = pl.DeviceIdType.MESH


def gather_kernel(
    x_ref, c_ref, g_ref, wg_ref, wu_ref, wd_ref,
    xo_ref, co_ref, go_ref, fg_ref, fu_ref, fd_ref,
    line_send, line_recv, pass_send, own_sem, w_send, w_recv, y_send, y_recv,
):
    p = lax.axis_index("expert")
    n = lax.axis_size("expert")
    steps = n // 2
    z, core = p // 2, p % 2
    j = lax.axis_index("dp")
    grp = lax.axis_index("groups")
    sib = {"expert": p + 1 - 2 * core}
    right, left = {"expert": p + 2}, {"expert": p - 2}
    across, other_group = {"dp": 1 - j}, {"groups": 1 - grp}
    tok = x_ref.shape[0]
    depth = wg_ref.shape[1]
    ff = wg_ref.shape[2]

    barrier = pltpu.get_barrier_semaphore()
    for device in (sib, across, other_group):
        pl.semaphore_signal(barrier, inc=1, device_id=device, device_id_type=MESH)

    @pl.when(z > 0)
    def _():
        pl.semaphore_signal(barrier, inc=1, device_id=left, device_id_type=MESH)

    @pl.when(z < steps - 1)
    def _():
        pl.semaphore_signal(barrier, inc=1, device_id=right, device_id_type=MESH)

    @pl.when((z == 0) | (z == steps - 1))
    def _():
        pl.semaphore_wait(barrier, 4)

    @pl.when((z > 0) & (z < steps - 1))
    def _():
        pl.semaphore_wait(barrier, 5)

    sources = (x_ref, c_ref, g_ref)
    lands = (xo_ref, co_ref, go_ref)

    def shard(a, q):
        return lands[a].at[pl.ds(pl.multiple_of(q * tok, tok), tok)]

    def line_copy(a, q, src, device, way):
        sems = pass_send.at[a, q] if way == 2 else line_send.at[a, way, q]
        return pltpu.make_async_remote_copy(
            src_ref=src, dst_ref=shard(a, q), send_sem=sems, recv_sem=line_recv.at[a, q],
            device_id=device, device_id_type=MESH,
        )

    half = ff // 2

    def pieces(src, full, m, part):
        def at(ref, e, own, jj):
            if m < 2:
                rows = depth // 2
                base = (0 if own else 1) * jj * depth + part * rows
                return ref.at[e, pl.ds(pl.multiple_of(base, rows), rows)]
            base = (0 if own else 1) * jj * depth
            return ref.at[e, pl.ds(part * half, half), pl.ds(pl.multiple_of(base, depth), depth)]
        return at

    shards_w = ((wg_ref, fg_ref), (wu_ref, fu_ref), (wd_ref, fd_ref))

    def w_copy(m, part):
        src, full = shards_w[m]
        at = pieces(src, full, m, part)
        k = 2 * m + part
        return pltpu.make_async_remote_copy(
            src_ref=at(src, grp, True, 0), dst_ref=at(full, grp, False, j),
            send_sem=w_send.at[k], recv_sem=w_recv.at[k], device_id=across, device_id_type=MESH,
        )

    def w_arrived(m, part):
        src, full = shards_w[m]
        at = pieces(src, full, m, part)
        k = 2 * m + part
        return pltpu.make_async_remote_copy(
            src_ref=at(src, grp, True, 0), dst_ref=at(full, grp, False, 1 - j),
            send_sem=w_send.at[k], recv_sem=w_recv.at[k], device_id=across, device_id_type=MESH,
        )

    def y_copy(m, part, e):
        src, full = shards_w[m]
        at = pieces(src, full, m, part)
        k = 2 * m + part
        return pltpu.make_async_remote_copy(
            src_ref=at(full, e, False, 1 - j), dst_ref=at(full, e, False, 1 - j),
            send_sem=y_send.at[k], recv_sem=y_recv.at[k], device_id=other_group,
            device_id_type=MESH,
        )

    for a in (2, 0, 1):
        @pl.when(z < steps - 1)
        def _(a=a):
            line_copy(a, p, sources[a], right, 0).start()

        @pl.when(z > 0)
        def _(a=a):
            line_copy(a, p, sources[a], left, 1).start()

    for m in range(3):
        for part in range(2):
            w_copy(m, part).start()
    for a in (2, 0, 1):
        line_copy(a, p, sources[a], sib, 2).start()

    own = [pltpu.make_async_copy(sources[a], shard(a, p), own_sem.at[a]) for a in range(3)]
    own.append(pltpu.make_async_copy(
        wg_ref, fg_ref.at[:, pl.ds(pl.multiple_of(j * depth, depth), depth)], own_sem.at[3]))
    own.append(pltpu.make_async_copy(
        wu_ref, fu_ref.at[:, pl.ds(pl.multiple_of(j * depth, depth), depth)], own_sem.at[4]))
    own.append(pltpu.make_async_copy(
        wd_ref, fd_ref.at[:, :, pl.ds(pl.multiple_of(j * depth, depth), depth)], own_sem.at[5]))
    for copy in own:
        copy.start()

    def relay(a, d):
        @pl.when(z - d >= 0)
        def _():
            q = p - 2 * d
            line_copy(a, q, shard(a, q), right, 0).wait_recv()

            @pl.when(z < steps - 1)
            def _():
                line_copy(a, q, shard(a, q), right, 0).start()

            line_copy(a, q, shard(a, q), sib, 2).start()

        @pl.when(z + d < steps)
        def _():
            q = p + 2 * d
            line_copy(a, q, shard(a, q), left, 1).wait_recv()

            @pl.when(z > 0)
            def _():
                line_copy(a, q, shard(a, q), left, 1).start()

            line_copy(a, q, shard(a, q), sib, 2).start()

    def carry(k):
        w_arrived(k // 2, k % 2).wait_recv()
        y_copy(k // 2, k % 2, grp).start()

    events = []
    for d in range(1, steps):
        for a in (2, 0, 1):
            events.append(("z", a, d))
    line_events = [e for e in events]
    weights_at = list(range(6))
    total = len(line_events)
    for i, (_, a, d) in enumerate(line_events):
        if weights_at and i % 3 != 0:
            carry(weights_at.pop(0))
        relay(a, d)
    while weights_at:
        carry(weights_at.pop(0))
    for k in range(6):
        y_copy(k // 2, k % 2, 1 - grp).wait_recv()
    for a in range(3):
        for zz in range(steps):
            q = 2 * zz + 1 - core
            line_copy(a, q, shard(a, q), sib, 2).wait_recv()
    for copy in own:
        copy.wait()
    for k in range(6):
        w_copy(k // 2, k % 2).wait_send()
        y_copy(k // 2, k % 2, grp).wait_send()
    for a in range(3):
        for zz in range(steps):
            q = 2 * zz + core
            line_copy(a, q, shard(a, q), sib, 2).wait_send()

            @pl.when((zz <= z) & (z < steps - 1))
            def _(a=a, q=q):
                line_copy(a, q, shard(a, q), right, 0).wait_send()

            @pl.when((zz >= z) & (z > 0))
            def _(a=a, q=q):
                line_copy(a, q, shard(a, q), left, 1).wait_send()


def gather_all(tokens, cotangent, dense, gate_matrix, up_weight, down_weight):
    n = lax.axis_size("expert")
    exp_dev, depth, ff = gate_matrix.shape
    rows, width = tokens.shape
    S = jax.ShapeDtypeStruct
    return pl.pallas_call(
        gather_kernel,
        out_shape=(
            S((n * rows, width), BF16), S((n * rows, width), BF16),
            S((n * rows, dense.shape[1]), BF16),
            S((exp_dev, 2 * depth, ff), BF16), S((exp_dev, 2 * depth, ff), BF16),
            S((exp_dev, ff, 2 * depth), BF16),
        ),
        in_specs=[pl.BlockSpec(memory_space=pl.ANY)] * 6,
        out_specs=[pl.BlockSpec(memory_space=pl.ANY)] * 6,
        scratch_shapes=[
            pltpu.SemaphoreType.DMA((3, 2, n)), pltpu.SemaphoreType.DMA((3, n)),
            pltpu.SemaphoreType.DMA((3, n)), pltpu.SemaphoreType.DMA((6,)),
            pltpu.SemaphoreType.DMA((6,)), pltpu.SemaphoreType.DMA((6,)),
            pltpu.SemaphoreType.DMA((6,)), pltpu.SemaphoreType.DMA((6,)),
        ],
        compiler_params=pltpu.CompilerParams(collective_id=0, has_side_effects=True),
        name="gather_all",
    )(tokens, cotangent, dense, gate_matrix, up_weight, down_weight)


def mm(a, b, dims):
    return lax.dot_general(a, b, (dims, ((), ())), preferred_element_type=F32)


def dispatch_body(tokens, expert_ids, gate_weights, cotangent, gate_matrix, up_weight, down_weight):
    tok_dev, top = expert_ids.shape
    exp_dev = up_weight.shape[0]
    n_peers = lax.axis_size("expert")
    experts = exp_dev * n_peers
    cap = min(tok_dev, tok_dev * top * 9 // (8 * experts))
    width = tokens.shape[1]
    flat_ids = expert_ids.reshape(-1)
    pairs = flat_ids.shape[0]
    onehot = (flat_ids[:, None] == jnp.arange(experts, dtype=jnp.int32)[None, :]).astype(jnp.int32)
    before = jnp.cumsum(onehot, axis=0) - onehot
    position = jnp.sum(before * onehot, axis=1)
    slot = flat_ids * cap + position
    owner = (
        jnp.full((experts * cap,), -1, jnp.int32).at[slot].set(jnp.arange(pairs, dtype=jnp.int32))
    )
    filled = owner >= 0
    safe_pair = jnp.maximum(owner, 0)
    token_row = safe_pair // top
    send_rows = jnp.where(filled[:, None], tokens[token_row], jnp.zeros((), tokens.dtype)).reshape(
        n_peers, exp_dev * cap, width
    )
    send_gate = jnp.where(
        filled, gate_weights.reshape(-1)[safe_pair], jnp.zeros((), gate_weights.dtype)
    ).reshape(n_peers, exp_dev * cap)
    send_grad = jnp.where(
        filled[:, None], cotangent[token_row], jnp.zeros((), cotangent.dtype)
    ).reshape(n_peers, exp_dev * cap, width)
    recv_rows, recv_gate = (
        lax.all_to_all(send_rows, "expert", split_axis=0, concat_axis=0, tiled=True),
        lax.all_to_all(send_gate, "expert", split_axis=0, concat_axis=0, tiled=True),
    )
    full_gate, full_up, full_down = (
        lax.all_gather(gate_matrix, "dp", axis=1, tiled=True),
        lax.all_gather(up_weight, "dp", axis=1, tiled=True),
        lax.all_gather(down_weight, "dp", axis=2, tiled=True),
    )
    rows_four = recv_rows.reshape(n_peers, exp_dev, cap, width)
    pre_gate = jnp.einsum(
        "slcd,ldf->slcf", rows_four, full_gate, preferred_element_type=jnp.float32
    )
    pre_up = jnp.einsum("slcd,ldf->slcf", rows_four, full_up, preferred_element_type=jnp.float32)
    sig = jax.nn.sigmoid(pre_gate)
    active = pre_gate * sig
    hidden = (active * pre_up).astype(jnp.bfloat16)
    recv_grad = lax.all_to_all(send_grad, "expert", split_axis=0, concat_axis=0, tiled=True)
    grad_four = recv_grad.reshape(n_peers, exp_dev, cap, width)
    gate_three = recv_gate.reshape(n_peers, exp_dev, cap).astype(jnp.float32)[..., None]
    back = jnp.einsum("slcd,lfd->slcf", grad_four, full_down, preferred_element_type=jnp.float32)
    gate_grad = jnp.sum(hidden.astype(jnp.float32) * back, axis=3).astype(jnp.bfloat16)
    d_hidden = gate_three * back
    d_gate = (d_hidden * pre_up * (sig * (1.0 + pre_gate * (1.0 - sig)))).astype(jnp.bfloat16)
    d_up = (d_hidden * active).astype(jnp.bfloat16)
    d_out = (gate_three * grad_four.astype(jnp.float32)).astype(jnp.bfloat16)
    both = jnp.einsum("slcf,ldf->slcd", d_gate, full_gate, preferred_element_type=jnp.float32)
    both = both + jnp.einsum("slcf,ldf->slcd", d_up, full_up, preferred_element_type=jnp.float32)
    d_rows = both.astype(jnp.bfloat16)
    ret_rows, ret_gate = (
        lax.all_to_all(
            d_rows.reshape(n_peers, exp_dev * cap, width),
            "expert",
            split_axis=0,
            concat_axis=0,
            tiled=True,
        ),
        lax.all_to_all(
            gate_grad.reshape(n_peers, exp_dev * cap),
            "expert",
            split_axis=0,
            concat_axis=0,
            tiled=True,
        ),
    )
    gate_term = jnp.einsum("slcd,slcf->ldf", rows_four, d_gate, preferred_element_type=jnp.float32)
    up_term = jnp.einsum("slcd,slcf->ldf", rows_four, d_up, preferred_element_type=jnp.float32)
    down_term = jnp.einsum("slcf,slcd->lfd", hidden, d_out, preferred_element_type=jnp.float32)
    gate_sum, up_sum, down_sum = (
        lax.psum_scatter(
            gate_term.astype(jnp.bfloat16), "dp", scatter_dimension=1, tiled=True
        ).astype(jnp.float32),
        lax.psum_scatter(
            up_term.astype(jnp.bfloat16), "dp", scatter_dimension=1, tiled=True
        ).astype(jnp.float32),
        lax.psum_scatter(
            down_term.astype(jnp.bfloat16), "dp", scatter_dimension=2, tiled=True
        ).astype(jnp.float32),
    )
    per_pair = ret_rows.reshape(experts * cap, width)[slot]
    grad_tokens = jnp.sum(per_pair.reshape(tok_dev, top, width).astype(jnp.float32), axis=1).astype(
        jnp.bfloat16
    )
    grad_gates = ret_gate.reshape(-1)[slot].reshape(tok_dev, top)
    return (
        grad_tokens,
        grad_gates,
        gate_sum.astype(jnp.bfloat16),
        up_sum.astype(jnp.bfloat16),
        down_sum.astype(jnp.bfloat16),
    )


def dense_body(tokens, expert_ids, gate_weights, cotangent, gate_matrix, up_weight, down_weight):
    tok_dev, top = expert_ids.shape
    width = tokens.shape[1]
    exp_dev, _, ff = up_weight.shape
    n_peers = lax.axis_size("expert")
    experts = exp_dev * n_peers
    me = lax.axis_index("expert")
    rows = tok_dev * n_peers

    chosen = expert_ids[:, :, None] == jnp.arange(experts, dtype=jnp.int32)[None, None, :]
    dense = jnp.sum(jnp.where(chosen, gate_weights[:, :, None].astype(F32), 0.0), axis=1)
    dense = dense.astype(BF16)

    lanes = -(-experts // 128) * 128
    dense = jnp.pad(dense, ((0, 0), (0, lanes - experts)))
    x, c, gates, full_gate, full_up, full_down = gather_all(
        tokens, cotangent, dense, gate_matrix, up_weight, down_weight
    )
    mine = lax.dynamic_slice_in_dim(gates, me * exp_dev, exp_dev, axis=1).astype(F32)

    d_gates, d_ups, weighted, gate_grads = [], [], [], []
    for e in range(exp_dev):
        g = mine[:, e : e + 1]
        pre_gate = mm(x, full_gate[e], ((1,), (0,)))
        pre_up = mm(x, full_up[e], ((1,), (0,)))
        sig = jax.nn.sigmoid(pre_gate)
        active = pre_gate * sig
        hidden = (active * pre_up).astype(BF16).astype(F32)
        back = mm(c, full_down[e], ((1,), (1,)))
        gate_grads.append(jnp.sum(hidden * back, axis=1, keepdims=True))
        d_hidden = g * back
        d_gates.append((d_hidden * pre_up * (sig * (1.0 + pre_gate * (1.0 - sig)))).astype(BF16))
        d_ups.append((d_hidden * active).astype(BF16))
        weighted.append((g * hidden).astype(BF16))

    j = lax.axis_index("dp")

    def scatter(term, dim):
        half = term.shape[dim] // 2
        gone = lax.dynamic_slice_in_dim(term, (1 - j) * half, half, axis=dim).astype(BF16)
        kept = lax.dynamic_slice_in_dim(term, j * half, half, axis=dim).astype(BF16)
        came = lax.ppermute(gone, "dp", [(0, 1), (1, 0)])
        return (kept.astype(F32) + came.astype(F32)).astype(BF16)

    gate_out = scatter(jnp.stack([mm(x, d, ((0,), (0,))) for d in d_gates]), 1)
    up_out = scatter(jnp.stack([mm(x, d, ((0,), (0,))) for d in d_ups]), 1)
    down_out = scatter(jnp.stack([mm(h, c, ((0,), (0,))) for h in weighted]), 2)

    both = sum(mm(d_gates[e], full_gate[e], ((1,), (1,))) for e in range(exp_dev))
    both = both + sum(mm(d_ups[e], full_up[e], ((1,), (1,))) for e in range(exp_dev))
    gg = jnp.concatenate(gate_grads, axis=1).astype(BF16)
    grad_tokens = lax.psum_scatter(both.astype(BF16), "expert", scatter_dimension=0, tiled=True)
    back_gate = lax.all_to_all(
        gg.reshape(n_peers, tok_dev, exp_dev), "expert", split_axis=0, concat_axis=0, tiled=True
    )
    back_gate = back_gate.transpose(1, 0, 2).reshape(tok_dev, experts)
    grad_gates = jnp.sum(
        jnp.where(chosen, back_gate[:, None, :].astype(F32), 0.0), axis=2
    ).astype(BF16)
    return grad_tokens, grad_gates, gate_out, up_out, down_out


def body(*args):
    tok_dev, top = args[1].shape
    experts = args[5].shape[0] * lax.axis_size("expert")
    cap = min(tok_dev, tok_dev * top * 9 // (8 * experts))
    dense = tok_dev <= 2 * cap
    dense = dense and lax.axis_size("dp") == 2 and lax.axis_size("groups") == 2
    dense = dense and args[5].shape[0] == 2 and lax.axis_size("expert") >= 4
    return (dense_body if dense else dispatch_body)(*args)


def solution(mesh):
    placed = (
        P(("groups", "expert", "dp"), None),
        P(("groups", "expert", "dp"), None),
        P(("groups", "expert", "dp"), None),
        P(("groups", "expert", "dp"), None),
        P("expert", "dp", None),
        P("expert", "dp", None),
        P("expert", None, "dp"),
    )
    return jax.shard_map(
        body,
        mesh=mesh,
        in_specs=placed,
        out_specs=(
            P(("groups", "expert", "dp"), None),
            P(("groups", "expert", "dp"), None),
            P(("groups", "expert"), "dp", None),
            P(("groups", "expert"), "dp", None),
            P(("groups", "expert"), None, "dp"),
        ),
        check_vma=False,
    )
```

```python
import jax
import jax.numpy as jnp
from jax import lax
from jax.experimental import pallas as pl
from jax.experimental.pallas import tpu as pltpu
from jax.sharding import PartitionSpec as P

F32 = jnp.float32
BF16 = jnp.bfloat16


MESH = pl.DeviceIdType.MESH


def gather_kernel(
    x_ref, c_ref, g_ref, wg_ref, wu_ref, wd_ref,
    xo_ref, co_ref, go_ref, fg_ref, fu_ref, fd_ref,
    line_send, line_recv, pass_send, own_sem, w_send, w_recv, y_send, y_recv, in_sem,
    x_st, c_st, g_st, wg_st, wu_st, wd_st,
):
    p = lax.axis_index("expert")
    n = lax.axis_size("expert")
    steps = n // 2
    z, core = p // 2, p % 2
    j = lax.axis_index("dp")
    grp = lax.axis_index("groups")
    sib = {"expert": p + 1 - 2 * core}
    right, left = {"expert": p + 2}, {"expert": p - 2}
    across, other_group = {"dp": 1 - j}, {"groups": 1 - grp}
    tok = x_ref.shape[0]
    depth = wg_ref.shape[1]
    ff = wg_ref.shape[2]

    barrier = pltpu.get_barrier_semaphore()
    for device in (sib, across, other_group):
        pl.semaphore_signal(barrier, inc=1, device_id=device, device_id_type=MESH)

    @pl.when(z > 0)
    def _():
        pl.semaphore_signal(barrier, inc=1, device_id=left, device_id_type=MESH)

    @pl.when(z < steps - 1)
    def _():
        pl.semaphore_signal(barrier, inc=1, device_id=right, device_id_type=MESH)

    @pl.when((z == 0) | (z == steps - 1))
    def _():
        pl.semaphore_wait(barrier, 4)

    @pl.when((z > 0) & (z < steps - 1))
    def _():
        pl.semaphore_wait(barrier, 5)

    sources = (x_ref, c_ref, g_ref)
    lands = (xo_ref, co_ref, go_ref)

    def shard(a, q):
        return lands[a].at[pl.ds(pl.multiple_of(q * tok, tok), tok)]

    def line_copy(a, q, src, device, way):
        sems = pass_send.at[a, q] if way == 2 else line_send.at[a, way, q]
        return pltpu.make_async_remote_copy(
            src_ref=src, dst_ref=shard(a, q), send_sem=sems, recv_sem=line_recv.at[a, q],
            device_id=device, device_id_type=MESH,
        )

    half = ff // 2

    def pieces(src, full, m, part):
        def at(ref, e, own, jj):
            if m < 2:
                rows = depth // 2
                base = (0 if own else 1) * jj * depth + part * rows
                return ref.at[e, pl.ds(pl.multiple_of(base, rows), rows)]
            base = (0 if own else 1) * jj * depth
            return ref.at[e, pl.ds(part * half, half), pl.ds(pl.multiple_of(base, depth), depth)]
        return at

    shards_w = ((wg_ref, fg_ref), (wu_ref, fu_ref), (wd_ref, fd_ref))

    def w_copy(m, part):
        src, full = shards_w[m]
        at = pieces(src, full, m, part)
        k = 2 * m + part
        return pltpu.make_async_remote_copy(
            src_ref=at(src, grp, True, 0), dst_ref=at(full, grp, False, j),
            send_sem=w_send.at[k], recv_sem=w_recv.at[k], device_id=across, device_id_type=MESH,
        )

    def w_arrived(m, part):
        src, full = shards_w[m]
        at = pieces(src, full, m, part)
        k = 2 * m + part
        return pltpu.make_async_remote_copy(
            src_ref=at(src, grp, True, 0), dst_ref=at(full, grp, False, 1 - j),
            send_sem=w_send.at[k], recv_sem=w_recv.at[k], device_id=across, device_id_type=MESH,
        )

    def y_copy(m, part, e):
        src, full = shards_w[m]
        at = pieces(src, full, m, part)
        k = 2 * m + part
        return pltpu.make_async_remote_copy(
            src_ref=at(full, e, False, 1 - j), dst_ref=at(full, e, False, 1 - j),
            send_sem=y_send.at[k], recv_sem=y_recv.at[k], device_id=other_group,
            device_id_type=MESH,
        )

    for a in (2, 0, 1):
        @pl.when(z < steps - 1)
        def _(a=a):
            line_copy(a, p, sources[a], right, 0).start()

        @pl.when(z > 0)
        def _(a=a):
            line_copy(a, p, sources[a], left, 1).start()

    for m in range(3):
        for part in range(2):
            w_copy(m, part).start()
    for a in (2, 0, 1):
        line_copy(a, p, sources[a], sib, 2).start()

    here = pl.ds(pl.multiple_of(j * depth, depth), depth)
    stages = (x_st, c_st, g_st, wg_st, wu_st, wd_st)
    homes = (
        shard(0, p), shard(1, p), shard(2, p),
        fg_ref.at[:, here], fu_ref.at[:, here], fd_ref.at[:, :, here],
    )
    blocks = (x_ref, c_ref, g_ref, wg_ref, wu_ref, wd_ref)
    into = [pltpu.make_async_copy(blocks[i], stages[i], in_sem.at[i]) for i in range(6)]
    own = [pltpu.make_async_copy(stages[i], homes[i], own_sem.at[i]) for i in range(6)]
    for copy in into:
        copy.start()
    for i in range(6):
        into[i].wait()
        own[i].start()

    def relay(a, d):
        @pl.when(z - d >= 0)
        def _():
            q = p - 2 * d
            line_copy(a, q, shard(a, q), right, 0).wait_recv()

            @pl.when(z < steps - 1)
            def _():
                line_copy(a, q, shard(a, q), right, 0).start()

            line_copy(a, q, shard(a, q), sib, 2).start()

        @pl.when(z + d < steps)
        def _():
            q = p + 2 * d
            line_copy(a, q, shard(a, q), left, 1).wait_recv()

            @pl.when(z > 0)
            def _():
                line_copy(a, q, shard(a, q), left, 1).start()

            line_copy(a, q, shard(a, q), sib, 2).start()

    def carry(k):
        w_arrived(k // 2, k % 2).wait_recv()
        y_copy(k // 2, k % 2, grp).start()

    events = []
    for d in range(1, steps):
        for a in (2, 0, 1):
            events.append(("z", a, d))
    line_events = [e for e in events]
    weights_at = list(range(6))
    total = len(line_events)
    for i, (_, a, d) in enumerate(line_events):
        if weights_at and i % 3 != 0:
            carry(weights_at.pop(0))
        relay(a, d)
    while weights_at:
        carry(weights_at.pop(0))
    for k in range(6):
        y_copy(k // 2, k % 2, 1 - grp).wait_recv()
    for a in range(3):
        for zz in range(steps):
            q = 2 * zz + 1 - core
            line_copy(a, q, shard(a, q), sib, 2).wait_recv()
    for copy in own:
        copy.wait()
    for k in range(6):
        w_copy(k // 2, k % 2).wait_send()
        y_copy(k // 2, k % 2, grp).wait_send()
    for a in range(3):
        for zz in range(steps):
            q = 2 * zz + core
            line_copy(a, q, shard(a, q), sib, 2).wait_send()

            @pl.when((zz <= z) & (z < steps - 1))
            def _(a=a, q=q):
                line_copy(a, q, shard(a, q), right, 0).wait_send()

            @pl.when((zz >= z) & (z > 0))
            def _(a=a, q=q):
                line_copy(a, q, shard(a, q), left, 1).wait_send()


def gather_all(tokens, cotangent, dense, gate_matrix, up_weight, down_weight):
    n = lax.axis_size("expert")
    exp_dev, depth, ff = gate_matrix.shape
    rows, width = tokens.shape
    S = jax.ShapeDtypeStruct
    return pl.pallas_call(
        gather_kernel,
        out_shape=(
            S((n * rows, width), BF16), S((n * rows, width), BF16),
            S((n * rows, dense.shape[1]), BF16),
            S((exp_dev, 2 * depth, ff), BF16), S((exp_dev, 2 * depth, ff), BF16),
            S((exp_dev, ff, 2 * depth), BF16),
        ),
        in_specs=[pl.BlockSpec(memory_space=pl.ANY)] * 6,
        out_specs=[pl.BlockSpec(memory_space=pl.ANY)] * 6,
        scratch_shapes=[
            pltpu.SemaphoreType.DMA((3, 2, n)), pltpu.SemaphoreType.DMA((3, n)),
            pltpu.SemaphoreType.DMA((3, n)), pltpu.SemaphoreType.DMA((6,)),
            pltpu.SemaphoreType.DMA((6,)), pltpu.SemaphoreType.DMA((6,)),
            pltpu.SemaphoreType.DMA((6,)), pltpu.SemaphoreType.DMA((6,)),
            pltpu.SemaphoreType.DMA((6,)),
        ]
        + [
            pltpu.VMEM(v.shape, v.dtype)
            for v in (tokens, cotangent, dense, gate_matrix, up_weight, down_weight)
        ],
        compiler_params=pltpu.CompilerParams(
            collective_id=0, has_side_effects=True, vmem_limit_bytes=56 * 1024 * 1024
        ),
        name="gather_all",
    )(tokens, cotangent, dense, gate_matrix, up_weight, down_weight)


def mm(a, b, dims):
    return lax.dot_general(a, b, (dims, ((), ())), preferred_element_type=F32)


def dispatch_body(tokens, expert_ids, gate_weights, cotangent, gate_matrix, up_weight, down_weight):
    tok_dev, top = expert_ids.shape
    exp_dev = up_weight.shape[0]
    n_peers = lax.axis_size("expert")
    experts = exp_dev * n_peers
    cap = min(tok_dev, tok_dev * top * 9 // (8 * experts))
    width = tokens.shape[1]
    flat_ids = expert_ids.reshape(-1)
    pairs = flat_ids.shape[0]
    onehot = (flat_ids[:, None] == jnp.arange(experts, dtype=jnp.int32)[None, :]).astype(jnp.int32)
    before = jnp.cumsum(onehot, axis=0) - onehot
    position = jnp.sum(before * onehot, axis=1)
    slot = flat_ids * cap + position
    owner = (
        jnp.full((experts * cap,), -1, jnp.int32).at[slot].set(jnp.arange(pairs, dtype=jnp.int32))
    )
    filled = owner >= 0
    safe_pair = jnp.maximum(owner, 0)
    token_row = safe_pair // top
    send_rows = jnp.where(filled[:, None], tokens[token_row], jnp.zeros((), tokens.dtype)).reshape(
        n_peers, exp_dev * cap, width
    )
    send_gate = jnp.where(
        filled, gate_weights.reshape(-1)[safe_pair], jnp.zeros((), gate_weights.dtype)
    ).reshape(n_peers, exp_dev * cap)
    send_grad = jnp.where(
        filled[:, None], cotangent[token_row], jnp.zeros((), cotangent.dtype)
    ).reshape(n_peers, exp_dev * cap, width)
    recv_rows, recv_gate = (
        lax.all_to_all(send_rows, "expert", split_axis=0, concat_axis=0, tiled=True),
        lax.all_to_all(send_gate, "expert", split_axis=0, concat_axis=0, tiled=True),
    )
    full_gate, full_up, full_down = (
        lax.all_gather(gate_matrix, "dp", axis=1, tiled=True),
        lax.all_gather(up_weight, "dp", axis=1, tiled=True),
        lax.all_gather(down_weight, "dp", axis=2, tiled=True),
    )
    rows_four = recv_rows.reshape(n_peers, exp_dev, cap, width)
    pre_gate = jnp.einsum(
        "slcd,ldf->slcf", rows_four, full_gate, preferred_element_type=jnp.float32
    )
    pre_up = jnp.einsum("slcd,ldf->slcf", rows_four, full_up, preferred_element_type=jnp.float32)
    sig = jax.nn.sigmoid(pre_gate)
    active = pre_gate * sig
    hidden = (active * pre_up).astype(jnp.bfloat16)
    recv_grad = lax.all_to_all(send_grad, "expert", split_axis=0, concat_axis=0, tiled=True)
    grad_four = recv_grad.reshape(n_peers, exp_dev, cap, width)
    gate_three = recv_gate.reshape(n_peers, exp_dev, cap).astype(jnp.float32)[..., None]
    back = jnp.einsum("slcd,lfd->slcf", grad_four, full_down, preferred_element_type=jnp.float32)
    gate_grad = jnp.sum(hidden.astype(jnp.float32) * back, axis=3).astype(jnp.bfloat16)
    d_hidden = gate_three * back
    d_gate = (d_hidden * pre_up * (sig * (1.0 + pre_gate * (1.0 - sig)))).astype(jnp.bfloat16)
    d_up = (d_hidden * active).astype(jnp.bfloat16)
    d_out = (gate_three * grad_four.astype(jnp.float32)).astype(jnp.bfloat16)
    both = jnp.einsum("slcf,ldf->slcd", d_gate, full_gate, preferred_element_type=jnp.float32)
    both = both + jnp.einsum("slcf,ldf->slcd", d_up, full_up, preferred_element_type=jnp.float32)
    d_rows = both.astype(jnp.bfloat16)
    ret_rows, ret_gate = (
        lax.all_to_all(
            d_rows.reshape(n_peers, exp_dev * cap, width),
            "expert",
            split_axis=0,
            concat_axis=0,
            tiled=True,
        ),
        lax.all_to_all(
            gate_grad.reshape(n_peers, exp_dev * cap),
            "expert",
            split_axis=0,
            concat_axis=0,
            tiled=True,
        ),
    )
    gate_term = jnp.einsum("slcd,slcf->ldf", rows_four, d_gate, preferred_element_type=jnp.float32)
    up_term = jnp.einsum("slcd,slcf->ldf", rows_four, d_up, preferred_element_type=jnp.float32)
    down_term = jnp.einsum("slcf,slcd->lfd", hidden, d_out, preferred_element_type=jnp.float32)
    gate_sum, up_sum, down_sum = (
        lax.psum_scatter(
            gate_term.astype(jnp.bfloat16), "dp", scatter_dimension=1, tiled=True
        ).astype(jnp.float32),
        lax.psum_scatter(
            up_term.astype(jnp.bfloat16), "dp", scatter_dimension=1, tiled=True
        ).astype(jnp.float32),
        lax.psum_scatter(
            down_term.astype(jnp.bfloat16), "dp", scatter_dimension=2, tiled=True
        ).astype(jnp.float32),
    )
    per_pair = ret_rows.reshape(experts * cap, width)[slot]
    grad_tokens = jnp.sum(per_pair.reshape(tok_dev, top, width).astype(jnp.float32), axis=1).astype(
        jnp.bfloat16
    )
    grad_gates = ret_gate.reshape(-1)[slot].reshape(tok_dev, top)
    return (
        grad_tokens,
        grad_gates,
        gate_sum.astype(jnp.bfloat16),
        up_sum.astype(jnp.bfloat16),
        down_sum.astype(jnp.bfloat16),
    )


def dense_body(tokens, expert_ids, gate_weights, cotangent, gate_matrix, up_weight, down_weight):
    tok_dev, top = expert_ids.shape
    width = tokens.shape[1]
    exp_dev, _, ff = up_weight.shape
    n_peers = lax.axis_size("expert")
    experts = exp_dev * n_peers
    me = lax.axis_index("expert")
    rows = tok_dev * n_peers

    chosen = expert_ids[:, :, None] == jnp.arange(experts, dtype=jnp.int32)[None, None, :]
    dense = jnp.sum(jnp.where(chosen, gate_weights[:, :, None].astype(F32), 0.0), axis=1)
    dense = dense.astype(BF16)

    lanes = -(-experts // 128) * 128
    dense = jnp.pad(dense, ((0, 0), (0, lanes - experts)))
    x, c, gates, full_gate, full_up, full_down = gather_all(
        tokens, cotangent, dense, gate_matrix, up_weight, down_weight
    )
    mine = lax.dynamic_slice_in_dim(gates, me * exp_dev, exp_dev, axis=1).astype(F32)

    j = lax.axis_index("dp")
    depth = gate_matrix.shape[1]
    swap = [(0, 1), (1, 0)]

    def sides(v):
        return (
            lax.dynamic_slice_in_dim(v, (1 - j) * depth, depth, axis=1),
            lax.dynamic_slice_in_dim(v, j * depth, depth, axis=1),
        )

    x_gone, x_kept = sides(x)
    local = range(exp_dev)
    pre_gates = [mm(x, full_gate[e], ((1,), (0,))) for e in local]
    pre_ups = [mm(x, full_up[e], ((1,), (0,))) for e in local]
    sigs = [jax.nn.sigmoid(v) for v in pre_gates]
    actives = [v * s for v, s in zip(pre_gates, sigs)]
    hiddens = [(v * u).astype(BF16) for v, u in zip(actives, pre_ups)]
    weighted = [(mine[:, e : e + 1] * hiddens[e].astype(F32)).astype(BF16) for e in local]

    c_gone, c_kept = sides(c)
    down_gone = [mm(h, c_gone, ((0,), (0,))).astype(BF16) for h in weighted]
    down_came = [lax.ppermute(v, "dp", swap) for v in down_gone]
    c_back, _ = lax.optimization_barrier((c, down_gone))

    d_gates, d_ups, gate_grads = [], [], []
    for e in local:
        sig, active = sigs[e], actives[e]
        back = mm(c_back, full_down[e], ((1,), (1,)))
        gate_grads.append(jnp.sum(hiddens[e].astype(F32) * back, axis=1, keepdims=True))
        d_hidden = mine[:, e : e + 1] * back
        slope = sig * (1.0 + pre_gates[e] * (1.0 - sig))
        d_gates.append((d_hidden * pre_ups[e] * slope).astype(BF16))
        d_ups.append((d_hidden * active).astype(BF16))

    gate_gone = [mm(x_gone, d, ((0,), (0,))).astype(BF16) for d in d_gates]
    gate_came = [lax.ppermute(v, "dp", swap) for v in gate_gone]
    up_gone = [mm(x_gone, d, ((0,), (0,))).astype(BF16) for d in d_ups]
    up_came = [lax.ppermute(v, "dp", swap) for v in up_gone]
    d_gates_r, d_ups_r, _, first_came = lax.optimization_barrier(
        (d_gates, d_ups, (gate_gone, up_gone), down_came[0])
    )
    down_came[0] = first_came

    both = sum(mm(d_gates_r[e], full_gate[e], ((1,), (1,))) for e in local)
    both = (both + sum(mm(d_ups_r[e], full_up[e], ((1,), (1,))) for e in local)).astype(BF16)
    d_gates_k, d_ups_k, weighted_k, _ = lax.optimization_barrier((d_gates, d_ups, weighted, both))

    def settle(first, second, came):
        parts = [mm(a, b, ((0,), (0,))).astype(BF16).astype(F32) for a, b in zip(first, second)]
        return jnp.stack([(v + w.astype(F32)).astype(BF16) for v, w in zip(parts, came)])

    down_out = settle(weighted_k, [c_kept] * exp_dev, down_came)
    gate_out = settle([x_kept] * exp_dev, d_gates_k, gate_came)
    up_out = settle([x_kept] * exp_dev, d_ups_k, up_came)
    gg = jnp.concatenate(gate_grads, axis=1).astype(BF16)
    grad_tokens = lax.psum_scatter(both, "expert", scatter_dimension=0, tiled=True)
    back_gate = lax.all_to_all(
        gg.reshape(n_peers, tok_dev, exp_dev), "expert", split_axis=0, concat_axis=0, tiled=True
    )
    back_gate = back_gate.transpose(1, 0, 2).reshape(tok_dev, experts)
    grad_gates = jnp.sum(
        jnp.where(chosen, back_gate[:, None, :].astype(F32), 0.0), axis=2
    ).astype(BF16)
    return grad_tokens, grad_gates, gate_out, up_out, down_out


def body(*args):
    tok_dev, top = args[1].shape
    experts = args[5].shape[0] * lax.axis_size("expert")
    cap = min(tok_dev, tok_dev * top * 9 // (8 * experts))
    dense = tok_dev <= 2 * cap
    dense = dense and lax.axis_size("dp") == 2 and lax.axis_size("groups") == 2
    dense = dense and args[5].shape[0] == 2 and lax.axis_size("expert") >= 4
    return (dense_body if dense else dispatch_body)(*args)


def solution(mesh):
    placed = (
        P(("groups", "expert", "dp"), None),
        P(("groups", "expert", "dp"), None),
        P(("groups", "expert", "dp"), None),
        P(("groups", "expert", "dp"), None),
        P("expert", "dp", None),
        P("expert", "dp", None),
        P("expert", None, "dp"),
    )
    return jax.shard_map(
        body,
        mesh=mesh,
        in_specs=placed,
        out_specs=(
            P(("groups", "expert", "dp"), None),
            P(("groups", "expert", "dp"), None),
            P(("groups", "expert"), "dp", None),
            P(("groups", "expert"), "dp", None),
            P(("groups", "expert"), None, "dp"),
        ),
        check_vma=False,
    )
```

```python
import jax
import jax.numpy as jnp
from jax import lax
from jax.experimental import pallas as pl
from jax.experimental.pallas import tpu as pltpu
from jax.sharding import PartitionSpec as P

F32 = jnp.float32
BF16 = jnp.bfloat16


MESH = pl.DeviceIdType.MESH


def gather_kernel(
    x_ref, c_ref, g_ref, wg_ref, wu_ref, wd_ref,
    xo_ref, co_ref, go_ref, fg_ref, fu_ref, fd_ref,
    line_send, line_recv, pass_send, own_sem, w_send, w_recv, y_send, y_recv, in_sem,
    x_st, c_st, g_st, wg_st, wu_st, wd_st,
):
    p = lax.axis_index("expert")
    n = lax.axis_size("expert")
    steps = n // 2
    z, core = p // 2, p % 2
    j = lax.axis_index("dp")
    grp = lax.axis_index("groups")
    sib = {"expert": p + 1 - 2 * core}
    right, left = {"expert": p + 2}, {"expert": p - 2}
    across, other_group = {"dp": 1 - j}, {"groups": 1 - grp}
    tok = x_ref.shape[0]
    depth = wg_ref.shape[1]
    ff = wg_ref.shape[2]

    barrier = pltpu.get_barrier_semaphore()
    for device in (sib, across, other_group):
        pl.semaphore_signal(barrier, inc=1, device_id=device, device_id_type=MESH)

    @pl.when(z > 0)
    def _():
        pl.semaphore_signal(barrier, inc=1, device_id=left, device_id_type=MESH)

    @pl.when(z < steps - 1)
    def _():
        pl.semaphore_signal(barrier, inc=1, device_id=right, device_id_type=MESH)

    @pl.when((z == 0) | (z == steps - 1))
    def _():
        pl.semaphore_wait(barrier, 4)

    @pl.when((z > 0) & (z < steps - 1))
    def _():
        pl.semaphore_wait(barrier, 5)

    sources = (x_ref, c_ref, g_ref)
    lands = (xo_ref, co_ref, go_ref)

    def shard(a, q):
        return lands[a].at[pl.ds(pl.multiple_of(q * tok, tok), tok)]

    def line_copy(a, q, src, device, way):
        sems = pass_send.at[a, q] if way == 2 else line_send.at[a, way, q]
        return pltpu.make_async_remote_copy(
            src_ref=src, dst_ref=shard(a, q), send_sem=sems, recv_sem=line_recv.at[a, q],
            device_id=device, device_id_type=MESH,
        )

    half = ff // 2

    def pieces(src, full, m, part):
        def at(ref, e, own, jj):
            if m < 2:
                rows = depth // 2
                base = (0 if own else 1) * jj * depth + part * rows
                return ref.at[e, pl.ds(pl.multiple_of(base, rows), rows)]
            base = (0 if own else 1) * jj * depth
            return ref.at[e, pl.ds(part * half, half), pl.ds(pl.multiple_of(base, depth), depth)]
        return at

    shards_w = ((wg_ref, fg_ref), (wu_ref, fu_ref), (wd_ref, fd_ref))

    def w_copy(m, part):
        src, full = shards_w[m]
        at = pieces(src, full, m, part)
        k = 2 * m + part
        return pltpu.make_async_remote_copy(
            src_ref=at(src, grp, True, 0), dst_ref=at(full, grp, False, j),
            send_sem=w_send.at[k], recv_sem=w_recv.at[k], device_id=across, device_id_type=MESH,
        )

    def w_arrived(m, part):
        src, full = shards_w[m]
        at = pieces(src, full, m, part)
        k = 2 * m + part
        return pltpu.make_async_remote_copy(
            src_ref=at(src, grp, True, 0), dst_ref=at(full, grp, False, 1 - j),
            send_sem=w_send.at[k], recv_sem=w_recv.at[k], device_id=across, device_id_type=MESH,
        )

    def y_copy(m, part, e):
        src, full = shards_w[m]
        at = pieces(src, full, m, part)
        k = 2 * m + part
        return pltpu.make_async_remote_copy(
            src_ref=at(full, e, False, 1 - j), dst_ref=at(full, e, False, 1 - j),
            send_sem=y_send.at[k], recv_sem=y_recv.at[k], device_id=other_group,
            device_id_type=MESH,
        )

    for a in (2, 0, 1):
        @pl.when(z < steps - 1)
        def _(a=a):
            line_copy(a, p, sources[a], right, 0).start()

        @pl.when(z > 0)
        def _(a=a):
            line_copy(a, p, sources[a], left, 1).start()

    for m in range(3):
        for part in range(2):
            w_copy(m, part).start()
    for a in (2, 0, 1):
        line_copy(a, p, sources[a], sib, 2).start()

    here = pl.ds(pl.multiple_of(j * depth, depth), depth)
    stages = (x_st, c_st, g_st, wg_st, wu_st, wd_st)
    homes = (
        shard(0, p), shard(1, p), shard(2, p),
        fg_ref.at[:, here], fu_ref.at[:, here], fd_ref.at[:, :, here],
    )
    blocks = (x_ref, c_ref, g_ref, wg_ref, wu_ref, wd_ref)
    into = [pltpu.make_async_copy(blocks[i], stages[i], in_sem.at[i]) for i in range(6)]
    own = [pltpu.make_async_copy(stages[i], homes[i], own_sem.at[i]) for i in range(6)]
    for copy in into:
        copy.start()
    for i in range(6):
        into[i].wait()
        own[i].start()

    def relay(a, d):
        @pl.when(z - d >= 0)
        def _():
            q = p - 2 * d
            line_copy(a, q, shard(a, q), right, 0).wait_recv()

            @pl.when(z < steps - 1)
            def _():
                line_copy(a, q, shard(a, q), right, 0).start()

            line_copy(a, q, shard(a, q), sib, 2).start()

        @pl.when(z + d < steps)
        def _():
            q = p + 2 * d
            line_copy(a, q, shard(a, q), left, 1).wait_recv()

            @pl.when(z > 0)
            def _():
                line_copy(a, q, shard(a, q), left, 1).start()

            line_copy(a, q, shard(a, q), sib, 2).start()

    def carry(k):
        w_arrived(k // 2, k % 2).wait_recv()
        y_copy(k // 2, k % 2, grp).start()

    events = []
    for d in range(1, steps):
        for a in (2, 0, 1):
            events.append(("z", a, d))
    line_events = [e for e in events]
    weights_at = list(range(6))
    total = len(line_events)
    for i, (_, a, d) in enumerate(line_events):
        if weights_at and i % 3 != 0:
            carry(weights_at.pop(0))
        relay(a, d)
    while weights_at:
        carry(weights_at.pop(0))
    for k in range(6):
        y_copy(k // 2, k % 2, 1 - grp).wait_recv()
    for a in range(3):
        for zz in range(steps):
            q = 2 * zz + 1 - core
            line_copy(a, q, shard(a, q), sib, 2).wait_recv()
    for copy in own:
        copy.wait()
    for k in range(6):
        w_copy(k // 2, k % 2).wait_send()
        y_copy(k // 2, k % 2, grp).wait_send()
    for a in range(3):
        for zz in range(steps):
            q = 2 * zz + core
            line_copy(a, q, shard(a, q), sib, 2).wait_send()

            @pl.when((zz <= z) & (z < steps - 1))
            def _(a=a, q=q):
                line_copy(a, q, shard(a, q), right, 0).wait_send()

            @pl.when((zz >= z) & (z > 0))
            def _(a=a, q=q):
                line_copy(a, q, shard(a, q), left, 1).wait_send()


def gather_all(tokens, cotangent, dense, gate_matrix, up_weight, down_weight):
    n = lax.axis_size("expert")
    exp_dev, depth, ff = gate_matrix.shape
    rows, width = tokens.shape
    S = jax.ShapeDtypeStruct
    return pl.pallas_call(
        gather_kernel,
        out_shape=(
            S((n * rows, width), BF16), S((n * rows, width), BF16),
            S((n * rows, dense.shape[1]), BF16),
            S((exp_dev, 2 * depth, ff), BF16), S((exp_dev, 2 * depth, ff), BF16),
            S((exp_dev, ff, 2 * depth), BF16),
        ),
        in_specs=[pl.BlockSpec(memory_space=pl.ANY)] * 6,
        out_specs=[pl.BlockSpec(memory_space=pl.ANY)] * 6,
        scratch_shapes=[
            pltpu.SemaphoreType.DMA((3, 2, n)), pltpu.SemaphoreType.DMA((3, n)),
            pltpu.SemaphoreType.DMA((3, n)), pltpu.SemaphoreType.DMA((6,)),
            pltpu.SemaphoreType.DMA((6,)), pltpu.SemaphoreType.DMA((6,)),
            pltpu.SemaphoreType.DMA((6,)), pltpu.SemaphoreType.DMA((6,)),
            pltpu.SemaphoreType.DMA((6,)),
        ]
        + [
            pltpu.VMEM(v.shape, v.dtype)
            for v in (tokens, cotangent, dense, gate_matrix, up_weight, down_weight)
        ],
        compiler_params=pltpu.CompilerParams(
            collective_id=0, has_side_effects=True, vmem_limit_bytes=56 * 1024 * 1024
        ),
        name="gather_all",
    )(tokens, cotangent, dense, gate_matrix, up_weight, down_weight)


def mm(a, b, dims):
    return lax.dot_general(a, b, (dims, ((), ())), preferred_element_type=F32)


def dispatch_body(tokens, expert_ids, gate_weights, cotangent, gate_matrix, up_weight, down_weight):
    tok_dev, top = expert_ids.shape
    exp_dev = up_weight.shape[0]
    n_peers = lax.axis_size("expert")
    experts = exp_dev * n_peers
    cap = min(tok_dev, tok_dev * top * 9 // (8 * experts))
    width = tokens.shape[1]
    flat_ids = expert_ids.reshape(-1)
    pairs = flat_ids.shape[0]
    onehot = (flat_ids[:, None] == jnp.arange(experts, dtype=jnp.int32)[None, :]).astype(jnp.int32)
    before = jnp.cumsum(onehot, axis=0) - onehot
    position = jnp.sum(before * onehot, axis=1)
    slot = flat_ids * cap + position
    owner = (
        jnp.full((experts * cap,), -1, jnp.int32).at[slot].set(jnp.arange(pairs, dtype=jnp.int32))
    )
    filled = owner >= 0
    safe_pair = jnp.maximum(owner, 0)
    token_row = safe_pair // top
    send_rows = jnp.where(filled[:, None], tokens[token_row], jnp.zeros((), tokens.dtype)).reshape(
        n_peers, exp_dev * cap, width
    )
    send_gate = jnp.where(
        filled, gate_weights.reshape(-1)[safe_pair], jnp.zeros((), gate_weights.dtype)
    ).reshape(n_peers, exp_dev * cap)
    send_grad = jnp.where(
        filled[:, None], cotangent[token_row], jnp.zeros((), cotangent.dtype)
    ).reshape(n_peers, exp_dev * cap, width)
    recv_rows, recv_gate = (
        lax.all_to_all(send_rows, "expert", split_axis=0, concat_axis=0, tiled=True),
        lax.all_to_all(send_gate, "expert", split_axis=0, concat_axis=0, tiled=True),
    )
    full_gate, full_up, full_down = (
        lax.all_gather(gate_matrix, "dp", axis=1, tiled=True),
        lax.all_gather(up_weight, "dp", axis=1, tiled=True),
        lax.all_gather(down_weight, "dp", axis=2, tiled=True),
    )
    rows_four = recv_rows.reshape(n_peers, exp_dev, cap, width)
    pre_gate = jnp.einsum(
        "slcd,ldf->slcf", rows_four, full_gate, preferred_element_type=jnp.float32
    )
    pre_up = jnp.einsum("slcd,ldf->slcf", rows_four, full_up, preferred_element_type=jnp.float32)
    sig = jax.nn.sigmoid(pre_gate)
    active = pre_gate * sig
    hidden = (active * pre_up).astype(jnp.bfloat16)
    recv_grad = lax.all_to_all(send_grad, "expert", split_axis=0, concat_axis=0, tiled=True)
    grad_four = recv_grad.reshape(n_peers, exp_dev, cap, width)
    gate_three = recv_gate.reshape(n_peers, exp_dev, cap).astype(jnp.float32)[..., None]
    back = jnp.einsum("slcd,lfd->slcf", grad_four, full_down, preferred_element_type=jnp.float32)
    gate_grad = jnp.sum(hidden.astype(jnp.float32) * back, axis=3).astype(jnp.bfloat16)
    d_hidden = gate_three * back
    d_gate = (d_hidden * pre_up * (sig * (1.0 + pre_gate * (1.0 - sig)))).astype(jnp.bfloat16)
    d_up = (d_hidden * active).astype(jnp.bfloat16)
    d_out = (gate_three * grad_four.astype(jnp.float32)).astype(jnp.bfloat16)
    both = jnp.einsum("slcf,ldf->slcd", d_gate, full_gate, preferred_element_type=jnp.float32)
    both = both + jnp.einsum("slcf,ldf->slcd", d_up, full_up, preferred_element_type=jnp.float32)
    d_rows = both.astype(jnp.bfloat16)
    ret_rows, ret_gate = (
        lax.all_to_all(
            d_rows.reshape(n_peers, exp_dev * cap, width),
            "expert",
            split_axis=0,
            concat_axis=0,
            tiled=True,
        ),
        lax.all_to_all(
            gate_grad.reshape(n_peers, exp_dev * cap),
            "expert",
            split_axis=0,
            concat_axis=0,
            tiled=True,
        ),
    )
    gate_term = jnp.einsum("slcd,slcf->ldf", rows_four, d_gate, preferred_element_type=jnp.float32)
    up_term = jnp.einsum("slcd,slcf->ldf", rows_four, d_up, preferred_element_type=jnp.float32)
    down_term = jnp.einsum("slcf,slcd->lfd", hidden, d_out, preferred_element_type=jnp.float32)
    gate_sum, up_sum, down_sum = (
        lax.psum_scatter(
            gate_term.astype(jnp.bfloat16), "dp", scatter_dimension=1, tiled=True
        ).astype(jnp.float32),
        lax.psum_scatter(
            up_term.astype(jnp.bfloat16), "dp", scatter_dimension=1, tiled=True
        ).astype(jnp.float32),
        lax.psum_scatter(
            down_term.astype(jnp.bfloat16), "dp", scatter_dimension=2, tiled=True
        ).astype(jnp.float32),
    )
    per_pair = ret_rows.reshape(experts * cap, width)[slot]
    grad_tokens = jnp.sum(per_pair.reshape(tok_dev, top, width).astype(jnp.float32), axis=1).astype(
        jnp.bfloat16
    )
    grad_gates = ret_gate.reshape(-1)[slot].reshape(tok_dev, top)
    return (
        grad_tokens,
        grad_gates,
        gate_sum.astype(jnp.bfloat16),
        up_sum.astype(jnp.bfloat16),
        down_sum.astype(jnp.bfloat16),
    )


def dense_body(tokens, expert_ids, gate_weights, cotangent, gate_matrix, up_weight, down_weight):
    tok_dev, top = expert_ids.shape
    width = tokens.shape[1]
    exp_dev, _, ff = up_weight.shape
    n_peers = lax.axis_size("expert")
    experts = exp_dev * n_peers
    me = lax.axis_index("expert")
    rows = tok_dev * n_peers

    chosen = expert_ids[:, :, None] == jnp.arange(experts, dtype=jnp.int32)[None, None, :]
    dense = jnp.sum(jnp.where(chosen, gate_weights[:, :, None].astype(F32), 0.0), axis=1)
    dense = dense.astype(BF16)

    lanes = -(-experts // 128) * 128
    dense = jnp.pad(dense, ((0, 0), (0, lanes - experts)))
    x, c, gates, full_gate, full_up, full_down = gather_all(
        tokens, cotangent, dense, gate_matrix, up_weight, down_weight
    )
    mine = lax.dynamic_slice_in_dim(gates, me * exp_dev, exp_dev, axis=1).astype(F32)

    j = lax.axis_index("dp")
    depth = gate_matrix.shape[1]
    swap = [(0, 1), (1, 0)]

    def sides(v):
        return (
            lax.dynamic_slice_in_dim(v, (1 - j) * depth, depth, axis=1),
            lax.dynamic_slice_in_dim(v, j * depth, depth, axis=1),
        )

    x_gone, x_kept = sides(x)
    local = range(exp_dev)
    pre_gates = [mm(x, full_gate[e], ((1,), (0,))) for e in local]
    pre_ups = [mm(x, full_up[e], ((1,), (0,))) for e in local]
    sigs = [jax.nn.sigmoid(v) for v in pre_gates]
    actives = [v * s for v, s in zip(pre_gates, sigs)]
    hiddens = [(v * u).astype(BF16) for v, u in zip(actives, pre_ups)]
    weighted = [(mine[:, e : e + 1] * hiddens[e].astype(F32)).astype(BF16) for e in local]

    c_gone, c_kept = sides(c)
    down_gone = [mm(h, c_gone, ((0,), (0,))).astype(BF16) for h in weighted]
    down_came = [lax.ppermute(v, "dp", swap) for v in down_gone]
    c_back, _ = lax.optimization_barrier((c, down_gone))

    d_gates, d_ups, gate_grads = [], [], []
    for e in local:
        sig, active = sigs[e], actives[e]
        back = mm(c_back, full_down[e], ((1,), (1,)))
        gate_grads.append(jnp.sum(hiddens[e].astype(F32) * back, axis=1, keepdims=True))
        d_hidden = mine[:, e : e + 1] * back
        slope = sig * (1.0 + pre_gates[e] * (1.0 - sig))
        d_gates.append((d_hidden * pre_ups[e] * slope).astype(BF16))
        d_ups.append((d_hidden * active).astype(BF16))

    gate_gone = [mm(x_gone, d, ((0,), (0,))).astype(BF16) for d in d_gates]
    gate_came = [lax.ppermute(v, "dp", swap) for v in gate_gone]
    up_gone = [mm(x_gone, d, ((0,), (0,))).astype(BF16) for d in d_ups]
    up_came = [lax.ppermute(v, "dp", swap) for v in up_gone]
    d_gates_r, d_ups_r, _, first_came = lax.optimization_barrier(
        (d_gates, d_ups, (gate_gone, up_gone), down_came[0])
    )
    down_came[0] = first_came

    both = sum(mm(d_gates_r[e], full_gate[e], ((1,), (1,))) for e in local)
    d_ups_r, both, down_came[-1] = lax.optimization_barrier((d_ups_r, both, down_came[-1]))
    both = (both + sum(mm(d_ups_r[e], full_up[e], ((1,), (1,))) for e in local)).astype(BF16)
    both, gate_came[0] = lax.optimization_barrier((both, gate_came[0]))
    d_gates_k, d_ups_k, weighted_k, _ = lax.optimization_barrier((d_gates, d_ups, weighted, both))

    def settle(first, second, came):
        parts = [mm(a, b, ((0,), (0,))).astype(BF16).astype(F32) for a, b in zip(first, second)]
        return jnp.stack([(v + w.astype(F32)).astype(BF16) for v, w in zip(parts, came)])

    down_out = settle(weighted_k, [c_kept] * exp_dev, down_came)
    gate_out = settle([x_kept] * exp_dev, d_gates_k, gate_came)
    up_out = settle([x_kept] * exp_dev, d_ups_k, up_came)
    gg = jnp.concatenate(gate_grads, axis=1).astype(BF16)
    grad_tokens = lax.psum_scatter(both, "expert", scatter_dimension=0, tiled=True)
    back_gate = lax.all_to_all(
        gg.reshape(n_peers, tok_dev, exp_dev), "expert", split_axis=0, concat_axis=0, tiled=True
    )
    back_gate = back_gate.transpose(1, 0, 2).reshape(tok_dev, experts)
    grad_gates = jnp.sum(
        jnp.where(chosen, back_gate[:, None, :].astype(F32), 0.0), axis=2
    ).astype(BF16)
    return grad_tokens, grad_gates, gate_out, up_out, down_out


def body(*args):
    tok_dev, top = args[1].shape
    experts = args[5].shape[0] * lax.axis_size("expert")
    cap = min(tok_dev, tok_dev * top * 9 // (8 * experts))
    dense = tok_dev <= 2 * cap
    dense = dense and lax.axis_size("dp") == 2 and lax.axis_size("groups") == 2
    dense = dense and args[5].shape[0] == 2 and lax.axis_size("expert") >= 4
    return (dense_body if dense else dispatch_body)(*args)


def solution(mesh):
    placed = (
        P(("groups", "expert", "dp"), None),
        P(("groups", "expert", "dp"), None),
        P(("groups", "expert", "dp"), None),
        P(("groups", "expert", "dp"), None),
        P("expert", "dp", None),
        P("expert", "dp", None),
        P("expert", None, "dp"),
    )
    return jax.shard_map(
        body,
        mesh=mesh,
        in_specs=placed,
        out_specs=(
            P(("groups", "expert", "dp"), None),
            P(("groups", "expert", "dp"), None),
            P(("groups", "expert"), "dp", None),
            P(("groups", "expert"), "dp", None),
            P(("groups", "expert"), None, "dp"),
        ),
        check_vma=False,
    )
```
